32 devices in a mesh: groups: 2 (over y), tile: 16 (over z, x, core).
Axes of the slice: x: 2, y: 2, z: 4, core: 2. Of those that a mesh axis runs over, the one named last changes fastest.
Arguments:
- log_demand: float32 [512, 256], P(('groups', 'tile')), parts along dimension 0, may hold values from -3 to 0
- log_capacity: float32 [32, 256], P(('groups', 'tile')), parts along dimension 0, may hold values from -1 to 1
- warm_potential: float32 [32, 256], P(('groups', 'tile')), parts along dimension 0, may hold values from -4 to 4
- facility_xy: float32 [32, 2, 256], P('groups'), parts along dimension 0, may hold values from 0 to 1472
- pair_block: int32 [512, 16], P(('groups', 'tile')), parts along dimension 0, may hold values from 0 to 15, as said below
- pair_count: int32 [512], P(('groups', 'tile')), parts along dimension 0, may hold values from 1 to 16, as said below
Outputs:
- cell_potential: float32 [512, 256], P(('groups', 'tile')), parts along dimension 0
- facility_potential: float32 [32, 256], P(('groups', 'tile')), parts along dimension 0
The draws below stay inside these ranges and needn't reach their ends.
There are 2 independent parts, one for each index of `groups`. The reference program is written for one: setup_inputs(seed, part) draws one part's arguments, and reference() takes and returns one part's arrays. A program takes and returns all parts, laid end to end along the dimension named above; each array names one. Nothing has to cross between parts.
Inputs may be any that keep to these rules, and one draw needn't show every extreme that they name: `pair_count`: every tile has at least one active pair and some tile has 16. `pair_block`: the 16 slots of a tile name distinct blocks; slot 0 is the block of the tile's own tile row (block b belongs to tile row b); every slot's block b satisfies |b - floor(t / 16)| <= 16 for its tile t; slots at or beyond the tile's pair_count are ignored.
All inputs are finite; a program needn't handle non-finite values.
Results may differ from the reference program's by a relative error of at most 0.0003.
Values sent between devices are 32-bit elements; how exact they have to be, the bound alone decides.
A program may use at most 64 MiB of HBM per device.

```python
import jax
import jax.numpy as jnp
from jax import lax

TSIDE = 16
CELLS = 256
FACS = 256
TILE_COLS = 16
KSLOTS = 16
ITERS = 2
REACH = 64
SPAN = 16
TILES = 256
BLOCKS = 16


def draw_facility_xy(key, part):
    key_x, key_y = jax.random.split(key, 2)
    row_ids = jnp.arange(BLOCKS, dtype=jnp.int32)[:, None].astype(jnp.float32)
    across = jax.random.uniform(key_x, (BLOCKS, FACS), jnp.float32) * (TILE_COLS * TSIDE)
    along = (row_ids + jax.random.uniform(key_y, (BLOCKS, FACS), jnp.float32)) * TSIDE
    return jnp.stack([across, along], axis=1)


def draw_pair_block(key, part):
    row_ids = jnp.arange(TILES, dtype=jnp.int32) // TILE_COLS
    offsets = jnp.arange(2 * SPAN + 1, dtype=jnp.int32) - SPAN
    candidate = row_ids[:, None] + offsets[None, :]
    inside = (candidate >= 0) & (candidate < BLOCKS)
    jitter = jax.random.randint(key, (TILES, 2 * SPAN + 1), 0, 96)
    ranking = jnp.abs(offsets)[None, :] * 64 + jitter
    ranking = jnp.where(offsets[None, :] == 0, -1, ranking)
    ranking = jnp.where(inside, ranking, 100000)
    ranking = ranking * 64 + offsets[None, :] + SPAN
    order = jnp.argsort(ranking, axis=1, stable=True)
    return jnp.take_along_axis(candidate, order[:, :KSLOTS], axis=1).astype(jnp.int32)


def draw_pair_count(key, part):
    key_level, key_count, key_pick = jax.random.split(key, 3)
    level = jax.random.randint(key_level, (TILES // TILE_COLS,), 0, 4)
    ceiling = 1 + level * level * (KSLOTS - 1) // 9
    per_tile = jnp.repeat(ceiling, TILE_COLS)
    counts = 1 + jax.random.randint(key_count, (TILES,), 0, per_tile)
    picked = jax.random.randint(key_pick, (), 0, TILES)
    counts = jnp.where(jnp.arange(TILES, dtype=jnp.int32) == picked, KSLOTS, counts)
    return counts.astype(jnp.int32)


def block_levels(own_key, dims, cuts, smallest, largest):
    loudness = 1.0
    for position, blocks in cuts:
        heights = jax.random.uniform(jax.random.fold_in(jax.random.fold_in(own_key, 6), position), (blocks,), jnp.float32, smallest / len(cuts), largest / len(cuts))
        loudness = loudness * jnp.repeat(jnp.exp(heights), dims[position] // blocks).reshape((-1,) + (1,) * (len(dims) - 1 - position))
    return loudness


def scatter_about(key, extent, spread, most, pieces=(), held_as=jnp.bfloat16):
    loudness = block_levels(key, extent, pieces, -0.22, 0.18) if pieces else 1.0
    values = jax.random.normal(key, extent, jnp.float32) * spread * loudness
    return jnp.minimum(jnp.maximum(values, -most), most).astype(held_as)


def setup_inputs(seed: int = 0, part: int = 0) -> dict:
    keys = jax.random.split(jax.random.key(seed), 7)
    part_keys = jax.random.split(jax.random.fold_in(keys[6], part), 7)
    return {
        "log_demand": jnp.clip(-3.0 + 3.0 * jax.random.uniform(part_keys[0], (TILES, CELLS), jnp.float32) ** block_levels(part_keys[0], (TILES, CELLS), ((0, 16),), -0.2, 0.2), -3.0, 0.0),
        "log_capacity": jnp.clip(jax.random.uniform(part_keys[1], (BLOCKS, FACS), jnp.float32, -1.0, 1.0) * block_levels(part_keys[1], (BLOCKS, FACS), ((0, 16),), -0.4, 0.0), -1.0, 1.0),
        "warm_potential": scatter_about(part_keys[2], (BLOCKS, FACS), 1.0, 4.0, ((0, 16),), jnp.float32),
        "facility_xy": draw_facility_xy(jax.random.fold_in(jax.random.fold_in(keys[6], part), 71), part),
        "pair_block": draw_pair_block(jax.random.fold_in(jax.random.fold_in(keys[6], part), 71), part),
        "pair_count": draw_pair_count(jax.random.fold_in(jax.random.fold_in(keys[6], part), 71), part),
    }


LOWEST = -1.0e30


def cell_coords(tile_index):
    cell_ids = jnp.arange(TSIDE * TSIDE, dtype=jnp.int32)
    column = (tile_index % TILE_COLS) * TSIDE + cell_ids % TSIDE
    row_cell = (tile_index // TILE_COLS) * TSIDE + cell_ids // TSIDE
    return column.astype(jnp.float32) + 0.5, row_cell.astype(jnp.float32) + 0.5


def pair_cost(coord_x, coord_y, positions):
    delta_x = coord_x[None, :, None] - positions[:, 0, :][:, None, :]
    delta_y = coord_y[None, :, None] - positions[:, 1, :][:, None, :]
    return (delta_x * delta_x + delta_y * delta_y) / float(REACH * REACH)


def tile_pass(tile_index, demand_row, potentials, positions, active):
    coord_x, coord_y = cell_coords(tile_index)
    pair_costs = pair_cost(coord_x, coord_y, positions)
    scores = jnp.where(active[:, None, None], potentials[:, None, :] - pair_costs, LOWEST)
    row_top = jnp.max(scores, axis=(0, 2))
    row_sum = jnp.sum(jnp.exp(scores - row_top[None, :, None]), axis=(0, 2))
    cell_pot = demand_row - (row_top + jnp.log(row_sum))
    column_scores = cell_pot[None, :, None] - pair_costs
    col_top = jnp.max(column_scores, axis=1)
    col_sum = jnp.sum(jnp.exp(column_scores - col_top[:, None, :]), axis=1)
    col_top = jnp.where(active[:, None], col_top, LOWEST)
    col_sum = jnp.where(active[:, None], col_sum, 0.0)
    return cell_pot, col_top, col_sum


def reference(log_demand, log_capacity, warm_potential, facility_xy, pair_block, pair_count):
    slot_ids = jnp.arange(KSLOTS, dtype=jnp.int32)
    facility_pot = warm_potential
    cell_pot = log_demand
    for step_index in range(ITERS):
        current = facility_pot

        def one_tile(tile_index):
            active = slot_ids < pair_count[tile_index]
            blocks = pair_block[tile_index]
            return tile_pass(tile_index, log_demand[tile_index], current[blocks], facility_xy[blocks], active)

        cell_pot, col_top, col_sum = lax.map(one_tile, jnp.arange(TILES, dtype=jnp.int32))
        flat_ids = pair_block.reshape(-1)
        flat_top = col_top.reshape(-1, FACS)
        flat_sum = col_sum.reshape(-1, FACS)
        block_top = jnp.full((BLOCKS, FACS), LOWEST, jnp.float32).at[flat_ids].max(flat_top)
        block_sum = jnp.zeros((BLOCKS, FACS), jnp.float32).at[flat_ids].add(flat_sum * jnp.exp(flat_top - block_top[flat_ids]))
        facility_pot = log_capacity - (block_top + jnp.log(block_sum))
    return cell_pot, facility_pot
```

```python
import functools

import jax
import jax.numpy as jnp
from jax import lax
from jax.experimental import pallas as pl
from jax.experimental.pallas import tpu as pltpu
from jax.sharding import PartitionSpec as P

TSIDE = 16
TILE_COLS = 16
KSLOTS = 16
ITERS = 2
REACH = 64
SPAN = 16

CELLS = TSIDE * TSIDE
SCALE = 1.0 / float(REACH * REACH)
LOWEST = -1e30


def split(value):
    high = value.astype(jnp.bfloat16)
    low = (value - high.astype(jnp.float32)).astype(jnp.bfloat16)
    return high, low


def matmul(left, right_high, right_low, dims):
    rows = left.shape[0]
    high, low = split(left)
    dot = functools.partial(
        lax.dot_general, dimension_numbers=(dims, ((), ())), preferred_element_type=jnp.float32
    )
    both = dot(jnp.concatenate([high, low], axis=0), right_high)
    return both[:rows] + both[rows:] + dot(high, right_low)


def kernel(
    n,
    reach,
    window,
    demand_ref,
    cap_ref,
    warm_ref,
    xy_ref,
    pair_ref,
    count_ref,
    cell_ref,
    fac_ref,
    g_high,
    g_low,
    centre_cost,
    pots,
    part,
    land,
    mine,
    send_sem,
    recv_sem,
):
    me = lax.axis_index("tile")
    tiles = demand_ref.shape[0]
    facs = cap_ref.shape[1]
    everyone = window == n

    def first_of(device):
        return 0 if everyone else jnp.clip(device - reach, 0, n - window)

    first = first_of(me)
    here = me - first
    if everyone:
        offsets = list(range(1, n))
    else:
        offsets = [k for d in range(1, reach + 1) for k in (d, -d)]

    def each_peer(action):
        for index, offset in enumerate(offsets):
            if everyone:
                action(index, lax.rem(me + offset, n))
            else:
                peer = me + offset

                @pl.when((peer >= 0) & (peer < n))
                def _():
                    action(index, peer)

    if not everyone:
        pots[...] = jnp.zeros_like(pots)
        land[...] = jnp.full_like(land, LOWEST)

    barrier = pltpu.get_barrier_semaphore()
    each_peer(
        lambda index, peer: pl.semaphore_signal(
            barrier, inc=1, device_id={"tile": peer}, device_id_type=pl.DeviceIdType.MESH
        )
    )

    def outgoing(phase, source, target, index, peer):
        slot = me - first_of(peer)
        return pltpu.make_async_remote_copy(
            src_ref=source(peer),
            dst_ref=target.at[slot],
            send_sem=send_sem.at[phase, index],
            recv_sem=recv_sem.at[phase, slot],
            device_id={"tile": peer},
            device_id_type=pl.DeviceIdType.MESH,
        )

    def send(phase, source, target):
        each_peer(lambda index, peer: outgoing(phase, source, target, index, peer).start())

    def receive(phase, target):
        def one(index, peer):
            slot = peer - first
            pltpu.make_async_remote_copy(
                src_ref=target.at[slot],
                dst_ref=target.at[slot],
                send_sem=send_sem.at[phase, index],
                recv_sem=recv_sem.at[phase, slot],
                device_id={"tile": peer},
                device_id_type=pl.DeviceIdType.MESH,
            ).wait_recv()

        each_peer(one)

    def sent(phase, source, target):
        each_peer(lambda index, peer: outgoing(phase, source, target, index, peer).wait_send())

    tile_ids = lax.broadcasted_iota(jnp.int32, (tiles, 1), 0)
    counts = jnp.zeros((tiles, 1), jnp.int32)
    for tile in range(tiles):
        counts = jnp.where(tile_ids == tile, count_ref[tile], counts)
    slot_ids = lax.broadcasted_iota(jnp.int32, (tiles, KSLOTS), 1)
    active_blocks = jnp.where(slot_ids < counts, pair_ref[...], -1)

    centre_x = (tile_ids * TSIDE + TSIDE // 2).astype(jnp.float32)
    centre_y = (me * TSIDE + TSIDE // 2).astype(jnp.float32)
    side = lax.broadcasted_iota(jnp.int32, (TSIDE, 1), 0).astype(jnp.float32) - (TSIDE - 1) / 2

    pl.semaphore_wait(barrier, len(offsets) if everyone else jnp.minimum(me, reach) + jnp.minimum(n - 1 - me, reach))
    send(0, lambda peer: warm_ref, pots.at[0])
    pots[0, here] = warm_ref[...]

    @pl.loop(0, window)
    def _(slot):
        columns = pl.ds(pl.multiple_of(slot * facs, facs), facs)
        block = first + slot
        xy = xy_ref[block]
        fac_x, fac_y = xy[0:1], xy[1:2]
        hit = jnp.max(jnp.where(active_blocks == block, 1.0, 0.0), axis=1, keepdims=True)
        delta_x = centre_x - fac_x
        delta_y = centre_y - fac_y
        cost = (delta_x * delta_x + delta_y * delta_y) * SCALE
        centre_cost[:, columns] = jnp.where(hit > 0.0, cost, -LOWEST)
        along_x = jnp.exp((2 * SCALE) * side * fac_x)
        along_y = jnp.exp((2 * SCALE) * side * fac_y)
        for row in range(TSIDE):
            high, low = split(along_x * along_y[row : row + 1])
            rows = pl.ds(row * TSIDE, TSIDE)
            g_high[rows, columns] = high
            g_low[rows, columns] = low

    for step in range(ITERS):
        receive(2 * step, pots.at[step])
        potential = jnp.concatenate([pots[step, w] for w in range(window)], axis=1)
        scores = potential - centre_cost[...]
        top = jnp.max(scores, axis=1, keepdims=True)
        weights = jnp.exp(scores - top)
        sums = matmul(weights, g_high[...], g_low[...], ((1,), (1,)))
        rest = demand_ref[...] - (top + jnp.log(sums))
        if step == ITERS - 1:
            cell_ids = lax.broadcasted_iota(jnp.int32, (1, CELLS), 1)
            dx = (cell_ids % TSIDE).astype(jnp.float32) - (TSIDE - 1) / 2
            dy = (cell_ids // TSIDE).astype(jnp.float32) - (TSIDE - 1) / 2
            shift = (dx * (2.0 * centre_x + dx) + dy * (2.0 * centre_y + dy)) * SCALE
            cell_ref[...] = rest + shift
        rest_top = jnp.max(rest, axis=1, keepdims=True)
        column_sums = matmul(jnp.exp(rest - rest_top), g_high[...], g_low[...], ((1,), (0,)))
        column_scores = rest_top - centre_cost[...]
        column_top = jnp.max(column_scores, axis=0, keepdims=True)
        total = jnp.sum(jnp.exp(column_scores - column_top) * column_sums, axis=0, keepdims=True)
        partial = column_top + jnp.log(total)
        for w in range(window):
            part[step, w] = partial[:, w * facs : (w + 1) * facs]
        send(2 * step + 1, lambda peer: part.at[step, peer - first], land.at[step])
        land[step, here] = part[step, here]
        receive(2 * step + 1, land.at[step])
        parts = [land[step, w] for w in range(window)]
        own_top = functools.reduce(jnp.maximum, parts)
        own_sum = functools.reduce(jnp.add, [jnp.exp(p - own_top) for p in parts])
        facility = cap_ref[...] - (own_top + jnp.log(own_sum))
        if step == ITERS - 1:
            fac_ref[...] = facility
        else:
            mine[step] = facility
            send(2 * step + 2, lambda peer: mine.at[step], pots.at[step + 1])
            pots[step + 1, here] = facility

    sent(0, lambda peer: warm_ref, pots.at[0])
    for step in range(ITERS):
        sent(2 * step + 1, lambda peer: part.at[step, peer - first], land.at[step])
        if step < ITERS - 1:
            sent(2 * step + 2, lambda peer: mine.at[step], pots.at[step + 1])


def on_device(n, log_demand, log_capacity, warm_potential, facility_xy, pair_block, pair_count):
    tiles, cells = log_demand.shape
    blocks, facs = log_capacity.shape
    assert blocks == 1 and tiles == TILE_COLS and cells == CELLS
    reach = min(n - 1, SPAN)
    window = min(n, 2 * reach + 1)
    wide = window * facs
    vmem = pl.BlockSpec(memory_space=pltpu.VMEM)
    smem = pl.BlockSpec(memory_space=pltpu.SMEM)
    peers = n - 1 if window == n else 2 * reach
    return pl.pallas_call(
        functools.partial(kernel, n, reach, window),
        out_shape=(
            jax.ShapeDtypeStruct((tiles, cells), jnp.float32),
            jax.ShapeDtypeStruct((blocks, facs), jnp.float32),
        ),
        in_specs=[vmem] * 5 + [smem],
        out_specs=(vmem, vmem),
        scratch_shapes=[
            pltpu.VMEM((cells, wide), jnp.bfloat16),
            pltpu.VMEM((cells, wide), jnp.bfloat16),
            pltpu.VMEM((tiles, wide), jnp.float32),
            pltpu.VMEM((ITERS, window, 1, facs), jnp.float32),
            pltpu.VMEM((ITERS, window, 1, facs), jnp.float32),
            pltpu.VMEM((ITERS, window, 1, facs), jnp.float32),
            pltpu.VMEM((ITERS, 1, facs), jnp.float32),
            pltpu.SemaphoreType.DMA((2 * ITERS, peers)),
            pltpu.SemaphoreType.DMA((2 * ITERS, window)),
        ],
        compiler_params=pltpu.CompilerParams(
            collective_id=0, has_side_effects=True, vmem_limit_bytes=48 * 1024 * 1024
        ),
    )(log_demand, log_capacity, warm_potential, facility_xy, pair_block, pair_count)


def solution(mesh):
    placed = (
        P(("groups", "tile"), None),
        P(("groups", "tile"), None),
        P(("groups", "tile"), None),
        P("groups", None, None),
        P(("groups", "tile"), None),
        P(("groups", "tile")),
    )
    return jax.shard_map(
        functools.partial(on_device, mesh.shape["tile"]),
        mesh=mesh,
        in_specs=placed,
        out_specs=(P(("groups", "tile"), None), P(("groups", "tile"), None)),
        check_vma=False,
    )
```

```python
import functools

import jax
import jax.numpy as jnp
from jax import lax
from jax.experimental import pallas as pl
from jax.experimental.pallas import tpu as pltpu
from jax.sharding import PartitionSpec as P

TSIDE = 16
TILE_COLS = 16
KSLOTS = 16
ITERS = 2
REACH = 64
SPAN = 16

CELLS = TSIDE * TSIDE
SCALE = 1.0 / float(REACH * REACH)
LOWEST = -1e30


def split(value):
    high = value.astype(jnp.bfloat16)
    low = (value - high.astype(jnp.float32)).astype(jnp.bfloat16)
    return high, low


def matmul(left, right_high, right_low, dims):
    rows = left.shape[0]
    high, low = split(left)
    dot = functools.partial(
        lax.dot_general, dimension_numbers=(dims, ((), ())), preferred_element_type=jnp.float32
    )
    both = dot(jnp.concatenate([high, low], axis=0), right_high)
    return both[:rows] + both[rows:] + dot(high, right_low)


def kernel(
    n,
    reach,
    window,
    demand_ref,
    cap_ref,
    warm_ref,
    xy_ref,
    pair_ref,
    count_ref,
    cell_ref,
    fac_ref,
    demand,
    cap,
    warm,
    xy,
    pair,
    count,
    load_sem,
    g_high,
    g_low,
    centre_cost,
    pots,
    part,
    land,
    mine,
    send_sem,
    recv_sem,
):
    me = lax.axis_index("tile")
    tiles = demand_ref.shape[0]
    facs = cap_ref.shape[1]
    everyone = window == n

    def first_of(device):
        return 0 if everyone else jnp.clip(device - reach, 0, n - window)

    first = first_of(me)
    here = me - first
    if everyone:
        offsets = list(range(1, n))
    else:
        offsets = [k for d in range(1, reach + 1) for k in (d, -d)]

    def each_peer(action):
        for index, offset in enumerate(offsets):
            if everyone:
                action(index, lax.rem(me + offset, n))
            else:
                peer = me + offset

                @pl.when((peer >= 0) & (peer < n))
                def _():
                    action(index, peer)

    if not everyone:
        pots[...] = jnp.zeros_like(pots)
        land[...] = jnp.full_like(land, LOWEST)

    barrier = pltpu.get_barrier_semaphore()
    each_peer(
        lambda index, peer: pl.semaphore_signal(
            barrier, inc=1, device_id={"tile": peer}, device_id_type=pl.DeviceIdType.MESH
        )
    )

    loads = [
        pltpu.make_async_copy(source, target, load_sem.at[index])
        for index, (source, target) in enumerate(
            [
                (xy_ref, xy),
                (warm_ref, warm),
                (pair_ref, pair),
                (count_ref, count),
                (demand_ref, demand),
                (cap_ref, cap),
            ]
        )
    ]
    for load in loads:
        load.start()

    def copy_between(phase, source, target, index, slot, peer):
        return pltpu.make_async_remote_copy(
            src_ref=source,
            dst_ref=target.at[slot],
            send_sem=send_sem.at[phase, 0 if everyone else index],
            recv_sem=recv_sem.at[phase, 0 if everyone else slot],
            device_id={"tile": peer},
            device_id_type=pl.DeviceIdType.MESH,
        )

    def outgoing(phase, source, target, index, peer):
        return copy_between(phase, source(peer), target, index, me - first_of(peer), peer)

    def send(phase, source, target):
        each_peer(lambda index, peer: outgoing(phase, source, target, index, peer).start())

    def receive(phase, target):
        if everyone:
            landed = target.at[pl.ds(0, n - 1)]
            pltpu.make_async_copy(landed, landed, recv_sem.at[phase, 0]).wait()
        else:
            each_peer(
                lambda index, peer: copy_between(
                    phase, target.at[peer - first], target, index, peer - first, peer
                ).wait_recv()
            )

    def sent(phase, source, target):
        if everyone:
            gone = target.at[pl.ds(0, n - 1)]
            pltpu.make_async_copy(gone, gone, send_sem.at[phase, 0]).wait()
        else:
            each_peer(
                lambda index, peer: outgoing(phase, source, target, index, peer).wait_send()
            )

    tile_ids = lax.broadcasted_iota(jnp.int32, (tiles, 1), 0)
    centre_x = (tile_ids * TSIDE + TSIDE // 2).astype(jnp.float32)
    centre_y = (me * TSIDE + TSIDE // 2).astype(jnp.float32)
    side = lax.broadcasted_iota(jnp.int32, (TSIDE, 1), 0).astype(jnp.float32) - (TSIDE - 1) / 2

    def build(slots):
        for slot in slots:
            columns = slice(slot * facs, (slot + 1) * facs)
            place = xy[first + slot]
            along_x = jnp.exp((2 * SCALE) * side * place[0:1])
            along_y = jnp.exp((2 * SCALE) * side * place[1:2])
            for row in range(TSIDE):
                high, low = split(along_x * along_y[row : row + 1])
                rows = slice(row * TSIDE, (row + 1) * TSIDE)
                g_high[rows, columns] = high
                g_low[rows, columns] = low

    loads[0].wait()
    build(range(0, window // 2))
    loads[1].wait()
    pl.semaphore_wait(
        barrier,
        n - 1 if everyone else jnp.minimum(me, reach) + jnp.minimum(n - 1 - me, reach),
    )
    send(0, lambda peer: warm, pots.at[0])
    pots[0, here] = warm[...]
    build(range(window // 2, window))
    for load in loads[2:]:
        load.wait()

    lanes = lax.broadcasted_iota(jnp.int32, (tiles, tiles), 1)
    counts = jnp.sum(jnp.where(lanes == tile_ids, count[...], 0), axis=1, keepdims=True)
    slot_ids = lax.broadcasted_iota(jnp.int32, (tiles, KSLOTS), 1)
    active_blocks = jnp.where(slot_ids < counts, pair[...], -1)
    for slot in range(window):
        hit = jnp.where(active_blocks == first + slot, 1.0, 0.0)
        hit = jnp.max(hit, axis=1, keepdims=True)
        place = xy[first + slot]
        delta_x = centre_x - place[0:1]
        delta_y = centre_y - place[1:2]
        cost = (delta_x * delta_x + delta_y * delta_y) * SCALE
        centre_cost[:, slot * facs : (slot + 1) * facs] = jnp.where(hit > 0.0, cost, -LOWEST)

    for step in range(ITERS):
        receive(2 * step, pots.at[step])
        potential = jnp.concatenate([pots[step, w] for w in range(window)], axis=1)
        scores = potential - centre_cost[...]
        top = jnp.max(scores, axis=1, keepdims=True)
        weights = jnp.exp(scores - top)
        sums = matmul(weights, g_high[...], g_low[...], ((1,), (1,)))
        rest = demand[...] - (top + jnp.log(sums))
        if step == ITERS - 1:
            cell_ids = lax.broadcasted_iota(jnp.int32, (1, CELLS), 1)
            dx = (cell_ids % TSIDE).astype(jnp.float32) - (TSIDE - 1) / 2
            dy = (cell_ids // TSIDE).astype(jnp.float32) - (TSIDE - 1) / 2
            shift = (dx * (2.0 * centre_x + dx) + dy * (2.0 * centre_y + dy)) * SCALE
            cell_ref[...] = rest + shift
        rest_top = jnp.max(rest, axis=1, keepdims=True)
        column_sums = matmul(jnp.exp(rest - rest_top), g_high[...], g_low[...], ((1,), (0,)))
        column_scores = rest_top - centre_cost[...]
        column_top = jnp.max(column_scores, axis=0, keepdims=True)
        total = jnp.sum(jnp.exp(column_scores - column_top) * column_sums, axis=0, keepdims=True)
        partial = column_top + jnp.log(total)
        for w in range(window):
            part[step, w] = partial[:, w * facs : (w + 1) * facs]
        send(2 * step + 1, lambda peer: part.at[step, peer - first], land.at[step])
        land[step, here] = part[step, here]
        receive(2 * step + 1, land.at[step])
        parts = [land[step, w] for w in range(window)]
        own_top = functools.reduce(jnp.maximum, parts)
        own_sum = functools.reduce(jnp.add, [jnp.exp(p - own_top) for p in parts])
        facility = cap[...] - (own_top + jnp.log(own_sum))
        if step == ITERS - 1:
            fac_ref[...] = facility
        else:
            mine[step] = facility
            send(2 * step + 2, lambda peer: mine.at[step], pots.at[step + 1])
            pots[step + 1, here] = facility

    sent(0, lambda peer: warm, pots.at[0])
    for step in range(ITERS):
        sent(2 * step + 1, lambda peer: part.at[step, peer - first], land.at[step])
        if step < ITERS - 1:
            sent(2 * step + 2, lambda peer: mine.at[step], pots.at[step + 1])


def on_device(n, log_demand, log_capacity, warm_potential, facility_xy, pair_block, pair_count):
    tiles, cells = log_demand.shape
    blocks, facs = log_capacity.shape
    assert blocks == 1 and tiles == TILE_COLS and cells == CELLS
    reach = min(n - 1, SPAN)
    window = min(n, 2 * reach + 1)
    wide = window * facs
    vmem = pl.BlockSpec(memory_space=pltpu.VMEM)
    hbm = pl.BlockSpec(memory_space=pltpu.HBM)
    peers = n - 1 if window == n else 2 * reach
    return pl.pallas_call(
        functools.partial(kernel, n, reach, window),
        out_shape=(
            jax.ShapeDtypeStruct((tiles, cells), jnp.float32),
            jax.ShapeDtypeStruct((blocks, facs), jnp.float32),
        ),
        in_specs=[hbm] * 6,
        out_specs=(vmem, vmem),
        scratch_shapes=[
            pltpu.VMEM((tiles, cells), jnp.float32),
            pltpu.VMEM((blocks, facs), jnp.float32),
            pltpu.VMEM((blocks, facs), jnp.float32),
            pltpu.VMEM(facility_xy.shape, jnp.float32),
            pltpu.VMEM(pair_block.shape, jnp.int32),
            pltpu.VMEM((1, tiles), jnp.int32),
            pltpu.SemaphoreType.DMA((6,)),
            pltpu.VMEM((cells, wide), jnp.bfloat16),
            pltpu.VMEM((cells, wide), jnp.bfloat16),
            pltpu.VMEM((tiles, wide), jnp.float32),
            pltpu.VMEM((ITERS, window, 1, facs), jnp.float32),
            pltpu.VMEM((ITERS, window, 1, facs), jnp.float32),
            pltpu.VMEM((ITERS, window, 1, facs), jnp.float32),
            pltpu.VMEM((ITERS, 1, facs), jnp.float32),
            pltpu.SemaphoreType.DMA((2 * ITERS, peers)),
            pltpu.SemaphoreType.DMA((2 * ITERS, window)),
        ],
        compiler_params=pltpu.CompilerParams(
            collective_id=0, has_side_effects=True, vmem_limit_bytes=48 * 1024 * 1024
        ),
    )(log_demand, log_capacity, warm_potential, facility_xy, pair_block, pair_count[None, :])


def solution(mesh):
    placed = (
        P(("groups", "tile"), None),
        P(("groups", "tile"), None),
        P(("groups", "tile"), None),
        P("groups", None, None),
        P(("groups", "tile"), None),
        P(("groups", "tile")),
    )
    return jax.shard_map(
        functools.partial(on_device, mesh.shape["tile"]),
        mesh=mesh,
        in_specs=placed,
        out_specs=(P(("groups", "tile"), None), P(("groups", "tile"), None)),
        check_vma=False,
    )
```

```python
import functools

import jax
import jax.numpy as jnp
from jax import lax
from jax.experimental import pallas as pl
from jax.experimental.pallas import tpu as pltpu
from jax.sharding import PartitionSpec as P

TSIDE = 16
TILE_COLS = 16
KSLOTS = 16
ITERS = 2
REACH = 64
SPAN = 16

CELLS = TSIDE * TSIDE
SCALE = 1.0 / float(REACH * REACH)
LOWEST = -1e30


def split(value):
    high = value.astype(jnp.bfloat16)
    low = (value - high.astype(jnp.float32)).astype(jnp.bfloat16)
    return high, low


def dot(left, right, dims):
    return lax.dot_general(left, right, (dims, ((), ())), preferred_element_type=jnp.float32)


def over_facilities(weights, g_high, g_low):
    rows = weights.shape[0]
    high, low = split(weights)
    dims = ((1,), (1,))
    both = dot(g_high, jnp.concatenate([high, low], axis=0), dims).T
    return both[:rows] + both[rows:] + dot(g_low, high, dims).T


def over_cells(weights, g_high, g_low):
    rows = weights.shape[0]
    high, low = split(weights)
    dims = ((1,), (0,))
    both = dot(jnp.concatenate([high, low], axis=0), g_high, dims)
    return both[:rows] + both[rows:] + dot(high, g_low, dims)


def kernel(
    n,
    reach,
    window,
    demand_ref,
    cap_ref,
    warm_ref,
    xy_ref,
    pair_ref,
    count_ref,
    cell_ref,
    fac_ref,
    demand,
    cap,
    warm,
    xy,
    pair,
    count,
    load_sem,
    g_high,
    g_low,
    centre_cost,
    pots,
    part,
    land,
    mine,
    send_sem,
    recv_sem,
):
    me = lax.axis_index("tile")
    tiles = demand_ref.shape[0]
    facs = cap_ref.shape[1]
    everyone = window == n

    def first_of(device):
        return 0 if everyone else jnp.clip(device - reach, 0, n - window)

    first = first_of(me)
    here = me - first
    if everyone:
        offsets = list(range(1, n))
    else:
        offsets = [k for d in range(1, reach + 1) for k in (d, -d)]

    def each_peer(action):
        for index, offset in enumerate(offsets):
            if everyone:
                action(index, lax.rem(me + offset, n))
            else:
                peer = me + offset

                @pl.when((peer >= 0) & (peer < n))
                def _():
                    action(index, peer)

    if not everyone:
        pots[...] = jnp.zeros_like(pots)
        land[...] = jnp.full_like(land, LOWEST)

    barrier = pltpu.get_barrier_semaphore()
    each_peer(
        lambda index, peer: pl.semaphore_signal(
            barrier, inc=1, device_id={"tile": peer}, device_id_type=pl.DeviceIdType.MESH
        )
    )

    loads = [
        pltpu.make_async_copy(source, target, load_sem.at[index])
        for index, (source, target) in enumerate(
            [
                (xy_ref, xy),
                (warm_ref, warm),
                (pair_ref, pair),
                (count_ref, count),
                (demand_ref, demand),
                (cap_ref, cap),
            ]
        )
    ]
    for load in loads:
        load.start()

    def copy_between(phase, source, target, index, slot, peer):
        return pltpu.make_async_remote_copy(
            src_ref=source,
            dst_ref=target.at[slot],
            send_sem=send_sem.at[phase, 0 if everyone else index],
            recv_sem=recv_sem.at[phase, 0 if everyone else slot],
            device_id={"tile": peer},
            device_id_type=pl.DeviceIdType.MESH,
        )

    def outgoing(phase, source, target, index, peer):
        return copy_between(phase, source(peer), target, index, me - first_of(peer), peer)

    def send(phase, source, target):
        each_peer(lambda index, peer: outgoing(phase, source, target, index, peer).start())

    def receive(phase, target):
        if everyone:
            landed = target.at[pl.ds(0, n - 1)]
            pltpu.make_async_copy(landed, landed, recv_sem.at[phase, 0]).wait()
        else:
            each_peer(
                lambda index, peer: copy_between(
                    phase, target.at[peer - first], target, index, peer - first, peer
                ).wait_recv()
            )

    def sent(phase, source, target):
        if everyone:
            gone = target.at[pl.ds(0, n - 1)]
            pltpu.make_async_copy(gone, gone, send_sem.at[phase, 0]).wait()
        else:
            each_peer(
                lambda index, peer: outgoing(phase, source, target, index, peer).wait_send()
            )

    tile_ids = lax.broadcasted_iota(jnp.int32, (tiles, 1), 0)
    centre_x = (tile_ids * TSIDE + TSIDE // 2).astype(jnp.float32)
    centre_y = (me * TSIDE + TSIDE // 2).astype(jnp.float32)
    side = lax.broadcasted_iota(jnp.int32, (TSIDE, 1), 0).astype(jnp.float32) - (TSIDE - 1) / 2

    def build(slots):
        for slot in slots:
            columns = slice(slot * facs, (slot + 1) * facs)
            place = xy[first + slot]
            along_x = jnp.exp((2 * SCALE) * side * place[0:1])
            along_y = jnp.exp((2 * SCALE) * side * place[1:2])
            for row in range(TSIDE):
                high, low = split(along_x * along_y[row : row + 1])
                rows = slice(row * TSIDE, (row + 1) * TSIDE)
                g_high[rows, columns] = high
                g_low[rows, columns] = low

    loads[0].wait()
    build(range(0, window // 2))
    loads[1].wait()
    pl.semaphore_wait(
        barrier,
        n - 1 if everyone else jnp.minimum(me, reach) + jnp.minimum(n - 1 - me, reach),
    )
    send(0, lambda peer: warm, pots.at[0])
    pots[0, here] = warm[...]
    build(range(window // 2, window))
    for load in loads[2:]:
        load.wait()

    lanes = lax.broadcasted_iota(jnp.int32, (tiles, tiles), 1)
    counts = jnp.sum(jnp.where(lanes == tile_ids, count[...], 0), axis=1, keepdims=True)
    slot_ids = lax.broadcasted_iota(jnp.int32, (tiles, KSLOTS), 1)
    active_blocks = jnp.where(slot_ids < counts, pair[...], -1)
    for slot in range(window):
        hit = jnp.where(active_blocks == first + slot, 1.0, 0.0)
        hit = jnp.max(hit, axis=1, keepdims=True)
        place = xy[first + slot]
        delta_x = centre_x - place[0:1]
        delta_y = centre_y - place[1:2]
        cost = (delta_x * delta_x + delta_y * delta_y) * SCALE
        centre_cost[:, slot * facs : (slot + 1) * facs] = jnp.where(hit > 0.0, cost, -LOWEST)

    for step in range(ITERS):
        receive(2 * step, pots.at[step])
        potential = jnp.concatenate([pots[step, w] for w in range(window)], axis=1)
        scores = potential - centre_cost[...]
        top = jnp.max(scores, axis=1, keepdims=True)
        weights = jnp.exp(scores - top)
        sums = over_facilities(weights, g_high[...], g_low[...])
        rest = demand[...] - (top + jnp.log(sums))
        if step == ITERS - 1:
            cell_ids = lax.broadcasted_iota(jnp.int32, (1, CELLS), 1)
            dx = (cell_ids % TSIDE).astype(jnp.float32) - (TSIDE - 1) / 2
            dy = (cell_ids // TSIDE).astype(jnp.float32) - (TSIDE - 1) / 2
            shift = (dx * (2.0 * centre_x + dx) + dy * (2.0 * centre_y + dy)) * SCALE
            cell_ref[...] = rest + shift
        rest_top = jnp.max(rest, axis=1, keepdims=True)
        column_sums = over_cells(jnp.exp(rest - rest_top), g_high[...], g_low[...])
        column_scores = rest_top - centre_cost[...]
        column_top = jnp.max(column_scores, axis=0, keepdims=True)
        total = jnp.sum(jnp.exp(column_scores - column_top) * column_sums, axis=0, keepdims=True)
        partial = column_top + jnp.log(total)
        for w in range(window):
            part[step, w] = partial[:, w * facs : (w + 1) * facs]
        send(2 * step + 1, lambda peer: part.at[step, peer - first], land.at[step])
        land[step, here] = part[step, here]
        receive(2 * step + 1, land.at[step])
        parts = [land[step, w] for w in range(window)]
        own_top = functools.reduce(jnp.maximum, parts)
        own_sum = functools.reduce(jnp.add, [jnp.exp(p - own_top) for p in parts])
        facility = cap[...] - (own_top + jnp.log(own_sum))
        if step == ITERS - 1:
            fac_ref[...] = facility
        else:
            mine[step] = facility
            send(2 * step + 2, lambda peer: mine.at[step], pots.at[step + 1])
            pots[step + 1, here] = facility

    sent(0, lambda peer: warm, pots.at[0])
    for step in range(ITERS):
        sent(2 * step + 1, lambda peer: part.at[step, peer - first], land.at[step])
        if step < ITERS - 1:
            sent(2 * step + 2, lambda peer: mine.at[step], pots.at[step + 1])


def on_device(n, log_demand, log_capacity, warm_potential, facility_xy, pair_block, pair_count):
    tiles, cells = log_demand.shape
    blocks, facs = log_capacity.shape
    assert blocks == 1 and tiles == TILE_COLS and cells == CELLS
    reach = min(n - 1, SPAN)
    window = min(n, 2 * reach + 1)
    wide = window * facs
    vmem = pl.BlockSpec(memory_space=pltpu.VMEM)
    hbm = pl.BlockSpec(memory_space=pltpu.HBM)
    peers = n - 1 if window == n else 2 * reach
    return pl.pallas_call(
        functools.partial(kernel, n, reach, window),
        out_shape=(
            jax.ShapeDtypeStruct((tiles, cells), jnp.float32),
            jax.ShapeDtypeStruct((blocks, facs), jnp.float32),
        ),
        in_specs=[hbm] * 6,
        out_specs=(vmem, vmem),
        scratch_shapes=[
            pltpu.VMEM((tiles, cells), jnp.float32),
            pltpu.VMEM((blocks, facs), jnp.float32),
            pltpu.VMEM((blocks, facs), jnp.float32),
            pltpu.VMEM(facility_xy.shape, jnp.float32),
            pltpu.VMEM(pair_block.shape, jnp.int32),
            pltpu.VMEM((1, tiles), jnp.int32),
            pltpu.SemaphoreType.DMA((6,)),
            pltpu.VMEM((cells, wide), jnp.bfloat16),
            pltpu.VMEM((cells, wide), jnp.bfloat16),
            pltpu.VMEM((tiles, wide), jnp.float32),
            pltpu.VMEM((ITERS, window, 1, facs), jnp.float32),
            pltpu.VMEM((ITERS, window, 1, facs), jnp.float32),
            pltpu.VMEM((ITERS, window, 1, facs), jnp.float32),
            pltpu.VMEM((ITERS, 1, facs), jnp.float32),
            pltpu.SemaphoreType.DMA((2 * ITERS, peers)),
            pltpu.SemaphoreType.DMA((2 * ITERS, window)),
        ],
        compiler_params=pltpu.CompilerParams(
            collective_id=0, has_side_effects=True, vmem_limit_bytes=64 * 1024 * 1024
        ),
    )(log_demand, log_capacity, warm_potential, facility_xy, pair_block, pair_count[None, :])


def solution(mesh):
    placed = (
        P(("groups", "tile"), None),
        P(("groups", "tile"), None),
        P(("groups", "tile"), None),
        P("groups", None, None),
        P(("groups", "tile"), None),
        P(("groups", "tile")),
    )
    return jax.shard_map(
        functools.partial(on_device, mesh.shape["tile"]),
        mesh=mesh,
        in_specs=placed,
        out_specs=(P(("groups", "tile"), None), P(("groups", "tile"), None)),
        check_vma=False,
    )
```

```python
import functools

import jax
import jax.numpy as jnp
from jax import lax
from jax.experimental import pallas as pl
from jax.experimental.pallas import tpu as pltpu
from jax.sharding import PartitionSpec as P

TSIDE = 16
TILE_COLS = 16
KSLOTS = 16
ITERS = 2
REACH = 64
SPAN = 16

CELLS = TSIDE * TSIDE
SCALE = 1.0 / float(REACH * REACH)
LOWEST = -1e30


def split(value):
    high = value.astype(jnp.bfloat16)
    low = (value - high.astype(jnp.float32)).astype(jnp.bfloat16)
    return high, low


def dot(left, right, dims):
    return lax.dot_general(left, right, (dims, ((), ())), preferred_element_type=jnp.float32)


def over_facilities(weights, g_high, g_low):
    rows = weights.shape[0]
    high, low = split(weights)
    dims = ((1,), (1,))
    both = dot(g_high, jnp.concatenate([high, low], axis=0), dims).T
    return both[:rows] + both[rows:] + dot(g_low, high, dims).T


def over_cells(weights, g_high, g_low):
    rows = weights.shape[0]
    high, low = split(weights)
    dims = ((1,), (0,))
    both = dot(jnp.concatenate([high, low], axis=0), g_high, dims)
    return both[:rows] + both[rows:] + dot(high, g_low, dims)


def kernel(
    n,
    reach,
    window,
    demand_ref,
    cap_ref,
    warm_ref,
    xy_ref,
    pair_ref,
    count_ref,
    cell_ref,
    fac_ref,
    demand,
    cap,
    warm,
    xy,
    pair,
    count,
    load_sem,
    g_high,
    g_low,
    centre_cost,
    pots,
    part,
    land,
    mine,
    send_sem,
    recv_sem,
):
    me = lax.axis_index("tile")
    tiles = demand_ref.shape[0]
    facs = cap_ref.shape[1]
    everyone = window == n

    def first_of(device):
        return 0 if everyone else jnp.clip(device - reach, 0, n - window)

    first = first_of(me)
    here = me - first
    offsets = [k for d in range(1, reach + 1) for k in (d, -d)]

    def each_peer(action):
        if everyone:

            @pl.loop(1, n)
            def _(offset):
                action(offset - 1, lax.rem(me + offset, n))

            return
        for index, offset in enumerate(offsets):
            peer = me + offset

            @pl.when((peer >= 0) & (peer < n))
            def _():
                action(index, peer)

    if not everyone:
        pots[...] = jnp.zeros_like(pots)
        land[...] = jnp.full_like(land, LOWEST)

    barrier = pltpu.get_barrier_semaphore()
    each_peer(
        lambda index, peer: pl.semaphore_signal(
            barrier, inc=1, device_id={"tile": peer}, device_id_type=pl.DeviceIdType.MESH
        )
    )

    loads = [
        pltpu.make_async_copy(source, target, load_sem.at[index])
        for index, (source, target) in enumerate(
            [
                (xy_ref, xy),
                (warm_ref, warm),
                (pair_ref, pair),
                (count_ref, count),
                (demand_ref, demand),
                (cap_ref, cap),
            ]
        )
    ]
    for load in loads:
        load.start()

    def copy_between(phase, source, target, index, slot, peer):
        return pltpu.make_async_remote_copy(
            src_ref=source,
            dst_ref=target.at[slot],
            send_sem=send_sem.at[phase, 0 if everyone else index],
            recv_sem=recv_sem.at[phase, 0 if everyone else slot],
            device_id={"tile": peer},
            device_id_type=pl.DeviceIdType.MESH,
        )

    def outgoing(phase, source, target, index, peer):
        return copy_between(phase, source(peer), target, index, me - first_of(peer), peer)

    def send(phase, source, target):
        each_peer(lambda index, peer: outgoing(phase, source, target, index, peer).start())

    def receive(phase, target):
        if everyone:
            landed = target.at[pl.ds(0, n - 1)]
            pltpu.make_async_copy(landed, landed, recv_sem.at[phase, 0]).wait()
        else:
            each_peer(
                lambda index, peer: copy_between(
                    phase, target.at[peer - first], target, index, peer - first, peer
                ).wait_recv()
            )

    def sent(phase, source, target):
        if everyone:
            gone = target.at[pl.ds(0, n - 1)]
            pltpu.make_async_copy(gone, gone, send_sem.at[phase, 0]).wait()
        else:
            each_peer(
                lambda index, peer: outgoing(phase, source, target, index, peer).wait_send()
            )

    tile_ids = lax.broadcasted_iota(jnp.int32, (tiles, 1), 0)
    centre_x = (tile_ids * TSIDE + TSIDE // 2).astype(jnp.float32)
    centre_y = (me * TSIDE + TSIDE // 2).astype(jnp.float32)
    side = lax.broadcasted_iota(jnp.int32, (TSIDE, 1), 0).astype(jnp.float32) - (TSIDE - 1) / 2

    def build(start, stop):
        @pl.loop(start, stop)
        def _(slot):
            columns = pl.ds(pl.multiple_of(slot * facs, facs), facs)
            place = xy[first + slot]
            hit = jnp.where(active_blocks == first + slot, 1.0, 0.0)
            hit = jnp.max(hit, axis=1, keepdims=True)
            delta_x = centre_x - place[0:1]
            delta_y = centre_y - place[1:2]
            cost = (delta_x * delta_x + delta_y * delta_y) * SCALE
            centre_cost[:, columns] = jnp.where(hit > 0.0, cost, -LOWEST)
            along_x = jnp.exp((2 * SCALE) * side * place[0:1])
            along_y = jnp.exp((2 * SCALE) * side * place[1:2])
            for row in range(TSIDE):
                high, low = split(along_x * along_y[row : row + 1])
                rows = slice(row * TSIDE, (row + 1) * TSIDE)
                g_high[rows, columns] = high
                g_low[rows, columns] = low

    for load in loads[:4]:
        load.wait()
    lanes = lax.broadcasted_iota(jnp.int32, (tiles, tiles), 1)
    counts = jnp.sum(jnp.where(lanes == tile_ids, count[...], 0), axis=1, keepdims=True)
    slot_ids = lax.broadcasted_iota(jnp.int32, (tiles, KSLOTS), 1)
    active_blocks = jnp.where(slot_ids < counts, pair[...], -1)

    build(0, window // 2)
    pl.semaphore_wait(
        barrier,
        n - 1 if everyone else jnp.minimum(me, reach) + jnp.minimum(n - 1 - me, reach),
    )
    send(0, lambda peer: warm, pots.at[0])
    pots[0, here] = warm[...]
    build(window // 2, window)
    for load in loads[4:]:
        load.wait()

    @pl.loop(0, ITERS)
    def _(step):
        receive(2 * step, pots.at[step])
        potential = jnp.concatenate([pots[step, w] for w in range(window)], axis=1)
        scores = potential - centre_cost[...]
        top = jnp.max(scores, axis=1, keepdims=True)
        weights = jnp.exp(scores - top)
        sums = over_facilities(weights, g_high[...], g_low[...])
        rest = demand[...] - (top + jnp.log(sums))

        @pl.when(step == ITERS - 1)
        def _():
            cell_ids = lax.broadcasted_iota(jnp.int32, (1, CELLS), 1)
            dx = (cell_ids % TSIDE).astype(jnp.float32) - (TSIDE - 1) / 2
            dy = (cell_ids // TSIDE).astype(jnp.float32) - (TSIDE - 1) / 2
            shift = (dx * (2.0 * centre_x + dx) + dy * (2.0 * centre_y + dy)) * SCALE
            cell_ref[...] = rest + shift

        rest_top = jnp.max(rest, axis=1, keepdims=True)
        column_sums = over_cells(jnp.exp(rest - rest_top), g_high[...], g_low[...])
        column_scores = rest_top - centre_cost[...]
        column_top = jnp.max(column_scores, axis=0, keepdims=True)
        total = jnp.sum(jnp.exp(column_scores - column_top) * column_sums, axis=0, keepdims=True)
        partial = column_top + jnp.log(total)
        for w in range(window):
            part[step, w] = partial[:, w * facs : (w + 1) * facs]
        send(2 * step + 1, lambda peer: part.at[step, peer - first], land.at[step])
        land[step, here] = part[step, here]
        receive(2 * step + 1, land.at[step])
        parts = [land[step, w] for w in range(window)]
        own_top = functools.reduce(jnp.maximum, parts)
        own_sum = functools.reduce(jnp.add, [jnp.exp(p - own_top) for p in parts])
        facility = cap[...] - (own_top + jnp.log(own_sum))

        @pl.when(step == ITERS - 1)
        def _():
            fac_ref[...] = facility

        @pl.when(step < ITERS - 1)
        def _():
            mine[step] = facility
            send(2 * step + 2, lambda peer: mine.at[step], pots.at[step + 1])
            pots[step + 1, here] = facility

    sent(0, lambda peer: warm, pots.at[0])
    for step in range(ITERS):
        sent(2 * step + 1, lambda peer: part.at[step, peer - first], land.at[step])
        if step < ITERS - 1:
            sent(2 * step + 2, lambda peer: mine.at[step], pots.at[step + 1])


def on_device(n, log_demand, log_capacity, warm_potential, facility_xy, pair_block, pair_count):
    tiles, cells = log_demand.shape
    blocks, facs = log_capacity.shape
    assert blocks == 1 and tiles == TILE_COLS and cells == CELLS
    reach = min(n - 1, SPAN)
    window = min(n, 2 * reach + 1)
    wide = window * facs
    vmem = pl.BlockSpec(memory_space=pltpu.VMEM)
    hbm = pl.BlockSpec(memory_space=pltpu.HBM)
    peers = n - 1 if window == n else 2 * reach
    return pl.pallas_call(
        functools.partial(kernel, n, reach, window),
        out_shape=(
            jax.ShapeDtypeStruct((tiles, cells), jnp.float32),
            jax.ShapeDtypeStruct((blocks, facs), jnp.float32),
        ),
        in_specs=[hbm] * 6,
        out_specs=(vmem, vmem),
        scratch_shapes=[
            pltpu.VMEM((tiles, cells), jnp.float32),
            pltpu.VMEM((blocks, facs), jnp.float32),
            pltpu.VMEM((blocks, facs), jnp.float32),
            pltpu.VMEM(facility_xy.shape, jnp.float32),
            pltpu.VMEM(pair_block.shape, jnp.int32),
            pltpu.VMEM((1, tiles), jnp.int32),
            pltpu.SemaphoreType.DMA((6,)),
            pltpu.VMEM((cells, wide), jnp.bfloat16),
            pltpu.VMEM((cells, wide), jnp.bfloat16),
            pltpu.VMEM((tiles, wide), jnp.float32),
            pltpu.VMEM((ITERS, window, 1, facs), jnp.float32),
            pltpu.VMEM((ITERS, window, 1, facs), jnp.float32),
            pltpu.VMEM((ITERS, window, 1, facs), jnp.float32),
            pltpu.VMEM((ITERS, 1, facs), jnp.float32),
            pltpu.SemaphoreType.DMA((2 * ITERS, peers)),
            pltpu.SemaphoreType.DMA((2 * ITERS, window)),
        ],
        compiler_params=pltpu.CompilerParams(
            collective_id=0, has_side_effects=True, vmem_limit_bytes=64 * 1024 * 1024
        ),
    )(log_demand, log_capacity, warm_potential, facility_xy, pair_block, pair_count[None, :])


def solution(mesh):
    placed = (
        P(("groups", "tile"), None),
        P(("groups", "tile"), None),
        P(("groups", "tile"), None),
        P("groups", None, None),
        P(("groups", "tile"), None),
        P(("groups", "tile")),
    )
    return jax.shard_map(
        functools.partial(on_device, mesh.shape["tile"]),
        mesh=mesh,
        in_specs=placed,
        out_specs=(P(("groups", "tile"), None), P(("groups", "tile"), None)),
        check_vma=False,
    )
```

```python
import functools

import jax
import jax.numpy as jnp
from jax import lax
from jax.experimental import pallas as pl
from jax.experimental.pallas import tpu as pltpu
from jax.sharding import PartitionSpec as P

TSIDE = 16
TILE_COLS = 16
KSLOTS = 16
ITERS = 2
REACH = 64
SPAN = 16

CELLS = TSIDE * TSIDE
SCALE = 1.0 / float(REACH * REACH)
LOWEST = -1e30


def split(value):
    high = value.astype(jnp.bfloat16)
    low = (value - high.astype(jnp.float32)).astype(jnp.bfloat16)
    return high, low


def dot(left, right, dims):
    return lax.dot_general(left, right, (dims, ((), ())), preferred_element_type=jnp.float32)


def over_facilities(weights, g_high, g_low):
    rows = weights.shape[0]
    high, low = split(weights)
    dims = ((1,), (1,))
    both = dot(g_high, jnp.concatenate([high, low], axis=0), dims).T
    return both[:rows] + both[rows:] + dot(g_low, high, dims).T


def over_cells(weights, g_high, g_low):
    rows = weights.shape[0]
    high, low = split(weights)
    dims = ((1,), (0,))
    both = dot(jnp.concatenate([high, low], axis=0), g_high, dims)
    return both[:rows] + both[rows:] + dot(high, g_low, dims)


def kernel(
    n,
    reach,
    window,
    demand_ref,
    cap_ref,
    warm_ref,
    xy_ref,
    pair_ref,
    count_ref,
    cell_ref,
    fac_ref,
    demand,
    cap,
    warm,
    xy,
    pair,
    count,
    load_sem,
    g_high,
    g_low,
    centre_cost,
    pots,
    part,
    land,
    mine,
    send_sem,
    recv_sem,
):
    me = lax.axis_index("tile")
    tiles = demand_ref.shape[0]
    facs = cap_ref.shape[1]
    everyone = window == n

    def first_of(device):
        return 0 if everyone else jnp.clip(device - reach, 0, n - window)

    first = first_of(me)
    here = me - first
    offsets = [k for d in range(1, reach + 1) for k in (d, -d)]

    def each_peer(action):
        if everyone:

            @pl.loop(1, n)
            def _(offset):
                action(offset - 1, lax.rem(me + offset, n))

            return
        for index, offset in enumerate(offsets):
            peer = me + offset

            @pl.when((peer >= 0) & (peer < n))
            def _():
                action(index, peer)

    if not everyone:
        pots[...] = jnp.zeros_like(pots)
        land[...] = jnp.full_like(land, LOWEST)

    barrier = pltpu.get_barrier_semaphore()
    each_peer(
        lambda index, peer: pl.semaphore_signal(
            barrier, inc=1, device_id={"tile": peer}, device_id_type=pl.DeviceIdType.MESH
        )
    )

    loads = [
        pltpu.make_async_copy(source, target, load_sem.at[index])
        for index, (source, target) in enumerate(
            [
                (xy_ref, xy),
                (warm_ref, warm),
                (pair_ref, pair),
                (count_ref, count),
                (demand_ref, demand),
                (cap_ref, cap),
            ]
        )
    ]
    for load in loads:
        load.start()

    def copy_between(phase, source, target, index, slot, peer):
        return pltpu.make_async_remote_copy(
            src_ref=source,
            dst_ref=target.at[slot],
            send_sem=send_sem.at[phase, 0 if everyone else index],
            recv_sem=recv_sem.at[phase, 0 if everyone else slot],
            device_id={"tile": peer},
            device_id_type=pl.DeviceIdType.MESH,
        )

    def outgoing(phase, source, target, index, peer):
        return copy_between(phase, source(peer), target, index, me - first_of(peer), peer)

    def send(phase, source, target):
        each_peer(lambda index, peer: outgoing(phase, source, target, index, peer).start())

    def receive(phase, target):
        if everyone:
            landed = target.at[pl.ds(0, n - 1)]
            pltpu.make_async_copy(landed, landed, recv_sem.at[phase, 0]).wait()
        else:
            each_peer(
                lambda index, peer: copy_between(
                    phase, target.at[peer - first], target, index, peer - first, peer
                ).wait_recv()
            )

    def sent(phase, source, target):
        if everyone:
            gone = target.at[pl.ds(0, n - 1)]
            pltpu.make_async_copy(gone, gone, send_sem.at[phase, 0]).wait()
        else:
            each_peer(
                lambda index, peer: outgoing(phase, source, target, index, peer).wait_send()
            )

    tile_ids = lax.broadcasted_iota(jnp.int32, (tiles, 1), 0)
    centre_x = (tile_ids * TSIDE + TSIDE // 2).astype(jnp.float32)
    centre_y = (me * TSIDE + TSIDE // 2).astype(jnp.float32)
    side = lax.broadcasted_iota(jnp.int32, (TSIDE, 1), 0).astype(jnp.float32) - (TSIDE - 1) / 2

    def build(start, stop):
        @pl.loop(start, stop)
        def _(slot):
            columns = pl.ds(pl.multiple_of(slot * facs, facs), facs)
            place = xy[first + slot]
            hit = jnp.where(active_blocks == first + slot, 1.0, 0.0)
            hit = jnp.max(hit, axis=1, keepdims=True)
            delta_x = centre_x - place[0:1]
            delta_y = centre_y - place[1:2]
            cost = (delta_x * delta_x + delta_y * delta_y) * SCALE
            centre_cost[:, columns] = jnp.where(hit > 0.0, cost, -LOWEST)
            along_x = jnp.exp((2 * SCALE) * side * place[0:1])
            along_y = jnp.exp((2 * SCALE) * side * place[1:2])
            for row in range(TSIDE):
                high, low = split(along_x * along_y[row : row + 1])
                rows = slice(row * TSIDE, (row + 1) * TSIDE)
                g_high[rows, columns] = high
                g_low[rows, columns] = low

    for load in loads[:4]:
        load.wait()
    lanes = lax.broadcasted_iota(jnp.int32, (tiles, tiles), 1)
    counts = jnp.sum(jnp.where(lanes == tile_ids, count[...], 0), axis=1, keepdims=True)
    slot_ids = lax.broadcasted_iota(jnp.int32, (tiles, KSLOTS), 1)
    active_blocks = jnp.where(slot_ids < counts, pair[...], -1)

    build(0, window // 2)
    pl.semaphore_wait(
        barrier,
        n - 1 if everyone else jnp.minimum(me, reach) + jnp.minimum(n - 1 - me, reach),
    )
    send(0, lambda peer: warm, pots.at[0])
    pots[0, here] = warm[...]
    build(window // 2, window)
    for load in loads[4:]:
        load.wait()

    @pl.loop(0, ITERS)
    def _(step):
        receive(2 * step, pots.at[step])
        potential = jnp.concatenate([pots[step, w] for w in range(window)], axis=1)
        scores = potential - centre_cost[...]
        top = jnp.max(scores, axis=1, keepdims=True)
        weights = jnp.exp(scores - top)
        sums = over_facilities(weights, g_high[...], g_low[...])
        rest = demand[...] - (top + jnp.log(sums))

        @pl.when(step == ITERS - 1)
        def _():
            cell_ids = lax.broadcasted_iota(jnp.int32, (1, CELLS), 1)
            dx = (cell_ids % TSIDE).astype(jnp.float32) - (TSIDE - 1) / 2
            dy = (cell_ids // TSIDE).astype(jnp.float32) - (TSIDE - 1) / 2
            shift = (dx * (2.0 * centre_x + dx) + dy * (2.0 * centre_y + dy)) * SCALE
            cell_ref[...] = rest + shift

        rest_top = jnp.max(rest, axis=1, keepdims=True)
        cell_weights = jnp.exp(rest - rest_top)
        for start, stop in ((0, window // 2), (window // 2, window)):
            columns = slice(start * facs, stop * facs)
            column_sums = over_cells(cell_weights, g_high[:, columns], g_low[:, columns])
            column_scores = rest_top - centre_cost[:, columns]
            column_top = jnp.max(column_scores, axis=0, keepdims=True)
            total = jnp.sum(
                jnp.exp(column_scores - column_top) * column_sums, axis=0, keepdims=True
            )
            partial = column_top + jnp.log(total)
            for w in range(start, stop):
                part[step, w] = partial[:, (w - start) * facs : (w - start + 1) * facs]
            if everyone:

                @pl.loop(start, stop)
                def _(peer):
                    @pl.when(peer != me)
                    def _():
                        source = part.at[step, peer]
                        copy_between(2 * step + 1, source, land.at[step], 0, me, peer).start()

        if not everyone:
            send(2 * step + 1, lambda peer: part.at[step, peer - first], land.at[step])
        land[step, here] = part[step, here]
        receive(2 * step + 1, land.at[step])
        parts = [land[step, w] for w in range(window)]
        own_top = functools.reduce(jnp.maximum, parts)
        own_sum = functools.reduce(jnp.add, [jnp.exp(p - own_top) for p in parts])
        facility = cap[...] - (own_top + jnp.log(own_sum))

        @pl.when(step == ITERS - 1)
        def _():
            fac_ref[...] = facility

        @pl.when(step < ITERS - 1)
        def _():
            mine[step] = facility
            send(2 * step + 2, lambda peer: mine.at[step], pots.at[step + 1])
            pots[step + 1, here] = facility

    sent(0, lambda peer: warm, pots.at[0])
    for step in range(ITERS):
        sent(2 * step + 1, lambda peer: part.at[step, peer - first], land.at[step])
        if step < ITERS - 1:
            sent(2 * step + 2, lambda peer: mine.at[step], pots.at[step + 1])


def on_device(n, log_demand, log_capacity, warm_potential, facility_xy, pair_block, pair_count):
    tiles, cells = log_demand.shape
    blocks, facs = log_capacity.shape
    assert blocks == 1 and tiles == TILE_COLS and cells == CELLS
    reach = min(n - 1, SPAN)
    window = min(n, 2 * reach + 1)
    wide = window * facs
    vmem = pl.BlockSpec(memory_space=pltpu.VMEM)
    hbm = pl.BlockSpec(memory_space=pltpu.HBM)
    peers = n - 1 if window == n else 2 * reach
    return pl.pallas_call(
        functools.partial(kernel, n, reach, window),
        out_shape=(
            jax.ShapeDtypeStruct((tiles, cells), jnp.float32),
            jax.ShapeDtypeStruct((blocks, facs), jnp.float32),
        ),
        in_specs=[hbm] * 6,
        out_specs=(vmem, vmem),
        scratch_shapes=[
            pltpu.VMEM((tiles, cells), jnp.float32),
            pltpu.VMEM((blocks, facs), jnp.float32),
            pltpu.VMEM((blocks, facs), jnp.float32),
            pltpu.VMEM(facility_xy.shape, jnp.float32),
            pltpu.VMEM(pair_block.shape, jnp.int32),
            pltpu.VMEM((1, tiles), jnp.int32),
            pltpu.SemaphoreType.DMA((6,)),
            pltpu.VMEM((cells, wide), jnp.bfloat16),
            pltpu.VMEM((cells, wide), jnp.bfloat16),
            pltpu.VMEM((tiles, wide), jnp.float32),
            pltpu.VMEM((ITERS, window, 1, facs), jnp.float32),
            pltpu.VMEM((ITERS, window, 1, facs), jnp.float32),
            pltpu.VMEM((ITERS, window, 1, facs), jnp.float32),
            pltpu.VMEM((ITERS, 1, facs), jnp.float32),
            pltpu.SemaphoreType.DMA((2 * ITERS, peers)),
            pltpu.SemaphoreType.DMA((2 * ITERS, window)),
        ],
        compiler_params=pltpu.CompilerParams(
            collective_id=0, has_side_effects=True, vmem_limit_bytes=64 * 1024 * 1024
        ),
    )(log_demand, log_capacity, warm_potential, facility_xy, pair_block, pair_count[None, :])


def solution(mesh):
    placed = (
        P(("groups", "tile"), None),
        P(("groups", "tile"), None),
        P(("groups", "tile"), None),
        P("groups", None, None),
        P(("groups", "tile"), None),
        P(("groups", "tile")),
    )
    return jax.shard_map(
        functools.partial(on_device, mesh.shape["tile"]),
        mesh=mesh,
        in_specs=placed,
        out_specs=(P(("groups", "tile"), None), P(("groups", "tile"), None)),
        check_vma=False,
    )
```

```python
import functools

import jax
import jax.numpy as jnp
from jax import lax
from jax.experimental import pallas as pl
from jax.experimental.pallas import tpu as pltpu
from jax.sharding import PartitionSpec as P

TSIDE = 16
TILE_COLS = 16
KSLOTS = 16
ITERS = 2
REACH = 64
SPAN = 16

CELLS = TSIDE * TSIDE
SCALE = 1.0 / float(REACH * REACH)
LOWEST = -1e30


def split(value):
    high = value.astype(jnp.bfloat16)
    low = (value - high.astype(jnp.float32)).astype(jnp.bfloat16)
    return high, low


def dot(left, right, dims):
    return lax.dot_general(left, right, (dims, ((), ())), preferred_element_type=jnp.float32)


def over_facilities(weights, g_high, g_low):
    rows = weights.shape[0]
    high, low = split(weights)
    dims = ((1,), (1,))
    both = dot(g_high, jnp.concatenate([high, low], axis=0), dims).T
    return both[:rows] + both[rows:] + dot(g_low, high, dims).T


def over_cells(weights, g_high, g_low):
    rows = weights.shape[0]
    high, low = split(weights)
    dims = ((1,), (0,))
    both = dot(jnp.concatenate([high, low], axis=0), g_high, dims)
    return both[:rows] + both[rows:] + dot(high, g_low, dims)


def kernel(
    n,
    reach,
    window,
    demand_ref,
    cap_ref,
    warm_ref,
    xy_ref,
    pair_ref,
    count_ref,
    cell_ref,
    fac_ref,
    demand,
    cap,
    warm,
    xy,
    pair,
    count,
    load_sem,
    g_high,
    g_low,
    centre_cost,
    pots,
    part,
    land,
    mine,
    send_sem,
    recv_sem,
):
    me = lax.axis_index("tile")
    tiles = demand_ref.shape[0]
    facs = cap_ref.shape[1]
    everyone = window == n

    def first_of(device):
        return 0 if everyone else jnp.clip(device - reach, 0, n - window)

    first = first_of(me)
    here = me - first
    offsets = [k for d in range(1, reach + 1) for k in (d, -d)]

    def each_peer(action):
        if everyone:

            @pl.loop(1, n)
            def _(offset):
                action(offset - 1, lax.rem(me + offset, n))

            return
        for index, offset in enumerate(offsets):
            peer = me + offset

            @pl.when((peer >= 0) & (peer < n))
            def _():
                action(index, peer)

    if not everyone:
        pots[...] = jnp.zeros_like(pots)
        land[...] = jnp.full_like(land, LOWEST)

    barrier = pltpu.get_barrier_semaphore()
    each_peer(
        lambda index, peer: pl.semaphore_signal(
            barrier, inc=1, device_id={"tile": peer}, device_id_type=pl.DeviceIdType.MESH
        )
    )

    loads = [
        pltpu.make_async_copy(source, target, load_sem.at[index])
        for index, (source, target) in enumerate(
            [
                (xy_ref, xy),
                (warm_ref, warm),
                (pair_ref, pair),
                (count_ref, count),
                (demand_ref, demand),
                (cap_ref, cap),
            ]
        )
    ]
    for load in loads:
        load.start()

    def copy_between(phase, source, target, index, slot, peer):
        return pltpu.make_async_remote_copy(
            src_ref=source,
            dst_ref=target.at[slot],
            send_sem=send_sem.at[phase, 0 if everyone else index],
            recv_sem=recv_sem.at[phase, 0 if everyone else slot],
            device_id={"tile": peer},
            device_id_type=pl.DeviceIdType.MESH,
        )

    def outgoing(phase, source, target, index, peer):
        return copy_between(phase, source(peer), target, index, me - first_of(peer), peer)

    def send(phase, source, target):
        each_peer(lambda index, peer: outgoing(phase, source, target, index, peer).start())

    def receive(phase, target):
        if everyone:
            landed = target.at[pl.ds(0, n - 1)]
            pltpu.make_async_copy(landed, landed, recv_sem.at[phase, 0]).wait()
        else:
            each_peer(
                lambda index, peer: copy_between(
                    phase, target.at[peer - first], target, index, peer - first, peer
                ).wait_recv()
            )

    def sent(phase, source, target):
        if everyone:
            gone = target.at[pl.ds(0, n - 1)]
            pltpu.make_async_copy(gone, gone, send_sem.at[phase, 0]).wait()
        else:
            each_peer(
                lambda index, peer: outgoing(phase, source, target, index, peer).wait_send()
            )

    tile_ids = lax.broadcasted_iota(jnp.int32, (tiles, 1), 0)
    centre_x = (tile_ids * TSIDE + TSIDE // 2).astype(jnp.float32)
    centre_y = (me * TSIDE + TSIDE // 2).astype(jnp.float32)
    side = lax.broadcasted_iota(jnp.int32, (TSIDE, 1), 0).astype(jnp.float32) - (TSIDE - 1) / 2

    def build(start, stop):
        for slot in range(start, stop):
            columns = slice(slot * facs, (slot + 1) * facs)
            place = xy[first + slot]
            hit = jnp.where(active_blocks == first + slot, 1.0, 0.0)
            hit = jnp.max(hit, axis=1, keepdims=True)
            delta_x = centre_x - place[0:1]
            delta_y = centre_y - place[1:2]
            cost = (delta_x * delta_x + delta_y * delta_y) * SCALE
            centre_cost[:, columns] = jnp.where(hit > 0.0, cost, -LOWEST)
            along_x = jnp.exp((2 * SCALE) * side * place[0:1])
            along_y = jnp.exp((2 * SCALE) * side * place[1:2])
            for row in range(TSIDE):
                high, low = split(along_x * along_y[row : row + 1])
                rows = slice(row * TSIDE, (row + 1) * TSIDE)
                g_high[rows, columns] = high
                g_low[rows, columns] = low

    for load in loads[:4]:
        load.wait()
    lanes = lax.broadcasted_iota(jnp.int32, (tiles, tiles), 1)
    counts = jnp.sum(jnp.where(lanes == tile_ids, count[...], 0), axis=1, keepdims=True)
    slot_ids = lax.broadcasted_iota(jnp.int32, (tiles, KSLOTS), 1)
    active_blocks = jnp.where(slot_ids < counts, pair[...], -1)

    build(0, window // 2)
    pl.semaphore_wait(
        barrier,
        n - 1 if everyone else jnp.minimum(me, reach) + jnp.minimum(n - 1 - me, reach),
    )
    send(0, lambda peer: warm, pots.at[0])
    pots[0, here] = warm[...]
    build(window // 2, window)
    for load in loads[4:]:
        load.wait()

    @pl.loop(0, ITERS)
    def _(step):
        receive(2 * step, pots.at[step])
        potential = jnp.concatenate([pots[step, w] for w in range(window)], axis=1)
        scores = potential - centre_cost[...]
        top = jnp.max(scores, axis=1, keepdims=True)
        weights = jnp.exp(scores - top)
        sums = over_facilities(weights, g_high[...], g_low[...])
        rest = demand[...] - (top + jnp.log(sums))

        @pl.when(step == ITERS - 1)
        def _():
            cell_ids = lax.broadcasted_iota(jnp.int32, (1, CELLS), 1)
            dx = (cell_ids % TSIDE).astype(jnp.float32) - (TSIDE - 1) / 2
            dy = (cell_ids // TSIDE).astype(jnp.float32) - (TSIDE - 1) / 2
            shift = (dx * (2.0 * centre_x + dx) + dy * (2.0 * centre_y + dy)) * SCALE
            cell_ref[...] = rest + shift

        rest_top = jnp.max(rest, axis=1, keepdims=True)
        cell_weights = jnp.exp(rest - rest_top)
        for start, stop in ((0, window // 2), (window // 2, window)):
            columns = slice(start * facs, stop * facs)
            column_sums = over_cells(cell_weights, g_high[:, columns], g_low[:, columns])
            column_scores = rest_top - centre_cost[:, columns]
            column_top = jnp.max(column_scores, axis=0, keepdims=True)
            total = jnp.sum(
                jnp.exp(column_scores - column_top) * column_sums, axis=0, keepdims=True
            )
            partial = column_top + jnp.log(total)
            for w in range(start, stop):
                part[step, w] = partial[:, (w - start) * facs : (w - start + 1) * facs]
            if everyone:

                @pl.loop(start, stop)
                def _(peer):
                    @pl.when(peer != me)
                    def _():
                        source = part.at[step, peer]
                        copy_between(2 * step + 1, source, land.at[step], 0, me, peer).start()

        if not everyone:
            send(2 * step + 1, lambda peer: part.at[step, peer - first], land.at[step])
        land[step, here] = part[step, here]
        receive(2 * step + 1, land.at[step])
        parts = [land[step, w] for w in range(window)]
        own_top = functools.reduce(jnp.maximum, parts)
        own_sum = functools.reduce(jnp.add, [jnp.exp(p - own_top) for p in parts])
        facility = cap[...] - (own_top + jnp.log(own_sum))

        @pl.when(step == ITERS - 1)
        def _():
            fac_ref[...] = facility

        @pl.when(step < ITERS - 1)
        def _():
            mine[step] = facility
            send(2 * step + 2, lambda peer: mine.at[step], pots.at[step + 1])
            pots[step + 1, here] = facility

    sent(0, lambda peer: warm, pots.at[0])
    for step in range(ITERS):
        sent(2 * step + 1, lambda peer: part.at[step, peer - first], land.at[step])
        if step < ITERS - 1:
            sent(2 * step + 2, lambda peer: mine.at[step], pots.at[step + 1])


def on_device(n, log_demand, log_capacity, warm_potential, facility_xy, pair_block, pair_count):
    tiles, cells = log_demand.shape
    blocks, facs = log_capacity.shape
    assert blocks == 1 and tiles == TILE_COLS and cells == CELLS
    reach = min(n - 1, SPAN)
    window = min(n, 2 * reach + 1)
    wide = window * facs
    vmem = pl.BlockSpec(memory_space=pltpu.VMEM)
    hbm = pl.BlockSpec(memory_space=pltpu.HBM)
    peers = n - 1 if window == n else 2 * reach
    return pl.pallas_call(
        functools.partial(kernel, n, reach, window),
        out_shape=(
            jax.ShapeDtypeStruct((tiles, cells), jnp.float32),
            jax.ShapeDtypeStruct((blocks, facs), jnp.float32),
        ),
        in_specs=[hbm] * 6,
        out_specs=(vmem, vmem),
        scratch_shapes=[
            pltpu.VMEM((tiles, cells), jnp.float32),
            pltpu.VMEM((blocks, facs), jnp.float32),
            pltpu.VMEM((blocks, facs), jnp.float32),
            pltpu.VMEM(facility_xy.shape, jnp.float32),
            pltpu.VMEM(pair_block.shape, jnp.int32),
            pltpu.VMEM((1, tiles), jnp.int32),
            pltpu.SemaphoreType.DMA((6,)),
            pltpu.VMEM((cells, wide), jnp.bfloat16),
            pltpu.VMEM((cells, wide), jnp.bfloat16),
            pltpu.VMEM((tiles, wide), jnp.float32),
            pltpu.VMEM((ITERS, window, 1, facs), jnp.float32),
            pltpu.VMEM((ITERS, window, 1, facs), jnp.float32),
            pltpu.VMEM((ITERS, window, 1, facs), jnp.float32),
            pltpu.VMEM((ITERS, 1, facs), jnp.float32),
            pltpu.SemaphoreType.DMA((2 * ITERS, peers)),
            pltpu.SemaphoreType.DMA((2 * ITERS, window)),
        ],
        compiler_params=pltpu.CompilerParams(
            collective_id=0, has_side_effects=True, vmem_limit_bytes=64 * 1024 * 1024
        ),
    )(log_demand, log_capacity, warm_potential, facility_xy, pair_block, pair_count[None, :])


def solution(mesh):
    placed = (
        P(("groups", "tile"), None),
        P(("groups", "tile"), None),
        P(("groups", "tile"), None),
        P("groups", None, None),
        P(("groups", "tile"), None),
        P(("groups", "tile")),
    )
    return jax.shard_map(
        functools.partial(on_device, mesh.shape["tile"]),
        mesh=mesh,
        in_specs=placed,
        out_specs=(P(("groups", "tile"), None), P(("groups", "tile"), None)),
        check_vma=False,
    )
```

```python
import functools

import jax
import jax.numpy as jnp
from jax import lax
from jax.experimental import pallas as pl
from jax.experimental.pallas import tpu as pltpu
from jax.sharding import PartitionSpec as P

TSIDE = 16
TILE_COLS = 16
KSLOTS = 16
ITERS = 2
REACH = 64
SPAN = 16

CELLS = TSIDE * TSIDE
SCALE = 1.0 / float(REACH * REACH)
LOWEST = -1e30


def split(value):
    high = value.astype(jnp.bfloat16)
    low = (value - high.astype(jnp.float32)).astype(jnp.bfloat16)
    return high, low


def dot(left, right, dims):
    return lax.dot_general(left, right, (dims, ((), ())), preferred_element_type=jnp.float32)


def over_facilities(weights, g_high, g_low):
    rows = weights.shape[0]
    high, low = split(weights)
    dims = ((1,), (1,))
    both = dot(g_high, jnp.concatenate([high, low], axis=0), dims).T
    return both[:rows] + both[rows:] + dot(g_low, high, dims).T


def over_cells(weights, g_high, g_low):
    rows = weights.shape[0]
    high, low = split(weights)
    dims = ((1,), (0,))
    both = dot(jnp.concatenate([high, low], axis=0), g_high, dims)
    return both[:rows] + both[rows:] + dot(high, g_low, dims)


def kernel(
    n,
    reach,
    window,
    demand_ref,
    cap_ref,
    warm_ref,
    xy_ref,
    pair_ref,
    count_ref,
    cell_ref,
    fac_ref,
    demand,
    cap,
    warm,
    xy,
    pair,
    count,
    load_sem,
    g_high,
    g_low,
    centre_cost,
    pots,
    part,
    land,
    mine,
    send_sem,
    recv_sem,
):
    me = lax.axis_index("tile")
    tiles = demand_ref.shape[0]
    facs = cap_ref.shape[1]
    everyone = window == n

    def first_of(device):
        return 0 if everyone else jnp.clip(device - reach, 0, n - window)

    first = first_of(me)
    here = me - first
    offsets = [k for d in range(1, reach + 1) for k in (d, -d)]

    def each_peer(action):
        if everyone:

            @pl.loop(1, n)
            def _(offset):
                action(offset - 1, lax.rem(me + offset, n))

            return
        for index, offset in enumerate(offsets):
            peer = me + offset

            @pl.when((peer >= 0) & (peer < n))
            def _():
                action(index, peer)

    if not everyone:
        pots[...] = jnp.zeros_like(pots)
        land[...] = jnp.full_like(land, LOWEST)

    barrier = pltpu.get_barrier_semaphore()
    each_peer(
        lambda index, peer: pl.semaphore_signal(
            barrier, inc=1, device_id={"tile": peer}, device_id_type=pl.DeviceIdType.MESH
        )
    )

    loads = [
        pltpu.make_async_copy(source, target, load_sem.at[index])
        for index, (source, target) in enumerate(
            [
                (xy_ref, xy),
                (warm_ref, warm),
                (pair_ref, pair),
                (count_ref, count),
                (demand_ref, demand),
                (cap_ref, cap),
            ]
        )
    ]
    for load in loads:
        load.start()

    def copy_between(phase, source, target, index, slot, peer):
        return pltpu.make_async_remote_copy(
            src_ref=source,
            dst_ref=target.at[slot],
            send_sem=send_sem.at[phase, 0 if everyone else index],
            recv_sem=recv_sem.at[phase, 0 if everyone else slot],
            device_id={"tile": peer},
            device_id_type=pl.DeviceIdType.MESH,
        )

    def outgoing(phase, source, target, index, peer):
        return copy_between(phase, source(peer), target, index, me - first_of(peer), peer)

    def send(phase, source, target):
        each_peer(lambda index, peer: outgoing(phase, source, target, index, peer).start())

    def receive(phase, target):
        if everyone:
            landed = target.at[pl.ds(0, n - 1)]
            pltpu.make_async_copy(landed, landed, recv_sem.at[phase, 0]).wait()
        else:
            each_peer(
                lambda index, peer: copy_between(
                    phase, target.at[peer - first], target, index, peer - first, peer
                ).wait_recv()
            )

    def sent(phase, source, target):
        if everyone:
            gone = target.at[pl.ds(0, n - 1)]
            pltpu.make_async_copy(gone, gone, send_sem.at[phase, 0]).wait()
        else:
            each_peer(
                lambda index, peer: outgoing(phase, source, target, index, peer).wait_send()
            )

    tile_ids = lax.broadcasted_iota(jnp.int32, (tiles, 1), 0)
    centre_x = (tile_ids * TSIDE + TSIDE // 2).astype(jnp.float32)
    centre_y = (me * TSIDE + TSIDE // 2).astype(jnp.float32)
    side = lax.broadcasted_iota(jnp.int32, (TSIDE, 1), 0).astype(jnp.float32) - (TSIDE - 1) / 2

    def build(start, stop):
        for slot in range(start, stop):
            columns = slice(slot * facs, (slot + 1) * facs)
            place = xy[first + slot]
            hit = jnp.where(active_blocks == first + slot, 1.0, 0.0)
            hit = jnp.max(hit, axis=1, keepdims=True)
            delta_x = centre_x - place[0:1]
            delta_y = centre_y - place[1:2]
            cost = (delta_x * delta_x + delta_y * delta_y) * SCALE
            centre_cost[:, columns] = jnp.where(hit > 0.0, cost, -LOWEST)
            along_x = jnp.exp((2 * SCALE) * side * place[0:1])
            along_y = jnp.exp((2 * SCALE) * side * place[1:2])
            for row in range(TSIDE):
                high, low = split(along_x * along_y[row : row + 1])
                rows = slice(row * TSIDE, (row + 1) * TSIDE)
                g_high[rows, columns] = high
                g_low[rows, columns] = low

    for load in loads[:4]:
        load.wait()
    lanes = lax.broadcasted_iota(jnp.int32, (tiles, tiles), 1)
    counts = jnp.sum(jnp.where(lanes == tile_ids, count[...], 0), axis=1, keepdims=True)
    slot_ids = lax.broadcasted_iota(jnp.int32, (tiles, KSLOTS), 1)
    active_blocks = jnp.where(slot_ids < counts, pair[...], -1)

    build(0, window // 4)
    pl.semaphore_wait(
        barrier,
        n - 1 if everyone else jnp.minimum(me, reach) + jnp.minimum(n - 1 - me, reach),
    )
    send(0, lambda peer: warm, pots.at[0])
    pots[0, here] = warm[...]
    build(window // 4, window)
    for load in loads[4:]:
        load.wait()

    @pl.loop(0, ITERS)
    def _(step):
        receive(2 * step, pots.at[step])
        potential = jnp.concatenate([pots[step, w] for w in range(window)], axis=1)
        scores = potential - centre_cost[...]
        top = jnp.max(scores, axis=1, keepdims=True)
        weights = jnp.exp(scores - top)
        sums = over_facilities(weights, g_high[...], g_low[...])
        rest = demand[...] - (top + jnp.log(sums))

        @pl.when(step == ITERS - 1)
        def _():
            cell_ids = lax.broadcasted_iota(jnp.int32, (1, CELLS), 1)
            dx = (cell_ids % TSIDE).astype(jnp.float32) - (TSIDE - 1) / 2
            dy = (cell_ids // TSIDE).astype(jnp.float32) - (TSIDE - 1) / 2
            shift = (dx * (2.0 * centre_x + dx) + dy * (2.0 * centre_y + dy)) * SCALE
            cell_ref[...] = rest + shift

        rest_top = jnp.max(rest, axis=1, keepdims=True)
        cell_weights = jnp.exp(rest - rest_top)
        for start, stop in ((0, window // 2), (window // 2, window)):
            columns = slice(start * facs, stop * facs)
            column_sums = over_cells(cell_weights, g_high[:, columns], g_low[:, columns])
            column_scores = rest_top - centre_cost[:, columns]
            column_top = jnp.max(column_scores, axis=0, keepdims=True)
            total = jnp.sum(
                jnp.exp(column_scores - column_top) * column_sums, axis=0, keepdims=True
            )
            partial = column_top + jnp.log(total)
            for w in range(start, stop):
                part[step, w] = partial[:, (w - start) * facs : (w - start + 1) * facs]
            if everyone:

                @pl.loop(start, stop)
                def _(peer):
                    @pl.when(peer != me)
                    def _():
                        source = part.at[step, peer]
                        copy_between(2 * step + 1, source, land.at[step], 0, me, peer).start()

        if not everyone:
            send(2 * step + 1, lambda peer: part.at[step, peer - first], land.at[step])
        land[step, here] = part[step, here]
        receive(2 * step + 1, land.at[step])
        parts = [land[step, w] for w in range(window)]
        own_top = functools.reduce(jnp.maximum, parts)
        own_sum = functools.reduce(jnp.add, [jnp.exp(p - own_top) for p in parts])
        facility = cap[...] - (own_top + jnp.log(own_sum))

        @pl.when(step == ITERS - 1)
        def _():
            fac_ref[...] = facility

        @pl.when(step < ITERS - 1)
        def _():
            mine[step] = facility
            send(2 * step + 2, lambda peer: mine.at[step], pots.at[step + 1])
            pots[step + 1, here] = facility

    sent(0, lambda peer: warm, pots.at[0])
    for step in range(ITERS):
        sent(2 * step + 1, lambda peer: part.at[step, peer - first], land.at[step])
        if step < ITERS - 1:
            sent(2 * step + 2, lambda peer: mine.at[step], pots.at[step + 1])


def on_device(n, log_demand, log_capacity, warm_potential, facility_xy, pair_block, pair_count):
    tiles, cells = log_demand.shape
    blocks, facs = log_capacity.shape
    assert blocks == 1 and tiles == TILE_COLS and cells == CELLS
    reach = min(n - 1, SPAN)
    window = min(n, 2 * reach + 1)
    wide = window * facs
    vmem = pl.BlockSpec(memory_space=pltpu.VMEM)
    hbm = pl.BlockSpec(memory_space=pltpu.HBM)
    peers = n - 1 if window == n else 2 * reach
    return pl.pallas_call(
        functools.partial(kernel, n, reach, window),
        out_shape=(
            jax.ShapeDtypeStruct((tiles, cells), jnp.float32),
            jax.ShapeDtypeStruct((blocks, facs), jnp.float32),
        ),
        in_specs=[hbm] * 6,
        out_specs=(vmem, vmem),
        scratch_shapes=[
            pltpu.VMEM((tiles, cells), jnp.float32),
            pltpu.VMEM((blocks, facs), jnp.float32),
            pltpu.VMEM((blocks, facs), jnp.float32),
            pltpu.VMEM(facility_xy.shape, jnp.float32),
            pltpu.VMEM(pair_block.shape, jnp.int32),
            pltpu.VMEM((1, tiles), jnp.int32),
            pltpu.SemaphoreType.DMA((6,)),
            pltpu.VMEM((cells, wide), jnp.bfloat16),
            pltpu.VMEM((cells, wide), jnp.bfloat16),
            pltpu.VMEM((tiles, wide), jnp.float32),
            pltpu.VMEM((ITERS, window, 1, facs), jnp.float32),
            pltpu.VMEM((ITERS, window, 1, facs), jnp.float32),
            pltpu.VMEM((ITERS, window, 1, facs), jnp.float32),
            pltpu.VMEM((ITERS, 1, facs), jnp.float32),
            pltpu.SemaphoreType.DMA((2 * ITERS, peers)),
            pltpu.SemaphoreType.DMA((2 * ITERS, window)),
        ],
        compiler_params=pltpu.CompilerParams(
            collective_id=0, has_side_effects=True, vmem_limit_bytes=64 * 1024 * 1024
        ),
    )(log_demand, log_capacity, warm_potential, facility_xy, pair_block, pair_count[None, :])


def solution(mesh):
    placed = (
        P(("groups", "tile"), None),
        P(("groups", "tile"), None),
        P(("groups", "tile"), None),
        P("groups", None, None),
        P(("groups", "tile"), None),
        P(("groups", "tile")),
    )
    return jax.shard_map(
        functools.partial(on_device, mesh.shape["tile"]),
        mesh=mesh,
        in_specs=placed,
        out_specs=(P(("groups", "tile"), None), P(("groups", "tile"), None)),
        check_vma=False,
    )
```
